32 devices in a mesh: dp: 2 (over y), corpus: 4 (over x, core), tensor: 4 (over z).
Axes of the slice: x: 2, y: 2, z: 4, core: 2. Of those that a mesh axis runs over, the one named last changes fastest.
Arguments:
- hidden: bfloat16 [4096, 4096], P(('dp', 'corpus')), may hold values from -6 to 6
- norm_gain: bfloat16 [4096], replicated, may hold values from 0.099609375 to 1.8984375
- query_weight: bfloat16 [4096, 4096], P('corpus', 'tensor'), may hold values from -0.1875 to 0.1875
- output_weight: bfloat16 [4096, 4096], P('tensor'), may hold values from -0.375 to 0.375
- cache: bfloat16 [2, 8192, 1024], P(None, 'corpus', 'tensor'), may hold values from -240 to 240
- pattern: int32 [32, 16], P(('dp', 'corpus')), may hold values from 0 to 63, as said below
Outputs:
- scored: bfloat16 [4096, 4096], P(('dp', 'corpus', 'tensor'))
The draws below stay inside these ranges and needn't reach their ends.
Inputs may be any that keep to these rules, and one draw needn't show every extreme that they name: Passage block j lies on index j // 16 of corpus. The 4 rows of pattern of one index of dp and corpus name blocks of exactly half of the indices of corpus, each of those exactly 32 times, repeats counted.
All inputs are finite; a program needn't handle non-finite values.
Results may differ from the reference program's by a relative error of at most 0.0075.
The reference program's roundings to bfloat16 on the way (of `normed`, `queries`, `probs` and `attended`) count: a program that leaves them out, or rounds other values in their place, can miss the bound.
Values may be sent and summed in bfloat16 or wider, within the bound.
A program may use at most 128 MiB of HBM per device.

```python
import math
import jax
import jax.numpy as jnp
from jax import lax

D = 4096
H = 32
KVH = 8
HD = 128
BLOCK = 128
CAND = 16
QB_DEV = 4
BLK_DEV = 16
QBLK = 32
QROWS = 4096
NBLK = 64
PASS = 8192
MOST = 32
N_DP = 2
N_CORPUS = 4


def draw_cache(key, part):
    first = jax.random.fold_in(key, 0)
    base = jax.random.truncated_normal(first, -4.0, 4.0, (2, PASS, KVH * HD), jnp.float32)
    return base.astype(jnp.bfloat16)


def draw_pattern(key, part):
    groups = N_DP * N_CORPUS
    slot_total = QB_DEV * CAND
    first, second, third = jax.random.split(key, 3)
    orders = jax.vmap(lambda sub: jax.random.permutation(sub, N_CORPUS))(jax.random.split(first, groups))
    sorted_owner = jnp.take(orders, jnp.arange(slot_total) // MOST, axis=1)
    shuffles = jax.vmap(lambda sub: jax.random.permutation(sub, slot_total))(jax.random.split(second, groups))
    owners = jnp.take_along_axis(sorted_owner, shuffles, axis=1)
    within = jax.random.randint(third, (groups, slot_total), 0, BLK_DEV)
    blocks = owners * BLK_DEV + within
    return blocks.reshape(groups * QB_DEV, CAND).astype(jnp.int32)


def level_of(rng, shape, cuts, least, high):
    def one(axis_at, shards_of):
        steps = jax.random.uniform(jax.random.fold_in(jax.random.fold_in(rng, 6), axis_at), (shards_of,), jnp.float32, least / len(cuts), high / len(cuts))
        return jnp.repeat(jnp.exp(steps), shape[axis_at] // shards_of).reshape((-1,) + (1,) * (len(shape) - axis_at - 1))

    loudness = one(*cuts[0])
    for cut in cuts[1:]:
        loudness = loudness * one(*cut)
    return loudness


def centred(own_key, extent, spread, most, cuts=(), held_as=jnp.bfloat16):
    array = spread * jax.random.normal(own_key, extent, jnp.float32)
    if cuts:
        array = array * level_of(own_key, extent, cuts, -0.22, 0.18)
    return jnp.clip(array, -most, most).astype(held_as)


def setup_inputs(seed: int = 0) -> dict:
    arg_keys = jax.random.split(jax.random.key(seed), 7)
    return {
        "hidden": centred(arg_keys[0], (QROWS, D), 1.0, 6.0, ((0, 8),)),
        "norm_gain": jnp.clip(1.0 + 0.18 * jax.random.normal(arg_keys[1], (D,), jnp.float32), 0.099609375, 1.8984375).astype(jnp.bfloat16),
        "query_weight": centred(arg_keys[2], (D, H * HD), (D // 4) ** -0.5, 0.1875, ((0, 4), (1, 4))),
        "output_weight": centred(arg_keys[3], (H * HD, D), (H * HD // 16) ** -0.5, 0.375, ((0, 4),)),
        "cache": draw_cache(jax.random.fold_in(arg_keys[6], 71), 0),
        "pattern": draw_pattern(jax.random.fold_in(arg_keys[6], 71), 0),
    }


def reference(hidden, norm_gain, query_weight, output_weight, cache, pattern):
    widened = hidden.astype(jnp.float32)
    meansq = lax.optimization_barrier(jnp.mean(widened * widened, axis=-1, keepdims=True))
    normed = (widened * lax.rsqrt(meansq + 1e-05) * norm_gain.astype(jnp.float32)).astype(jnp.bfloat16)
    factor = 1.0 / math.sqrt(HD)
    queries = (jnp.dot(normed, query_weight, preferred_element_type=jnp.float32) * factor).astype(jnp.bfloat16)
    query_tiles = queries.reshape(QBLK, BLOCK, KVH, H // KVH, HD)
    key_tiles = cache[0].reshape(NBLK, BLOCK, KVH, HD)
    value_tiles = cache[1].reshape(NBLK, BLOCK, KVH, HD)

    def attend(operands):
        query_tile, chosen = operands
        chosen = chosen.astype(jnp.int32)
        keys_here = jnp.take(key_tiles, chosen, axis=0).reshape(CAND * BLOCK, KVH, HD).astype(jnp.float32)
        values_here = jnp.take(value_tiles, chosen, axis=0).reshape(CAND * BLOCK, KVH, HD).astype(jnp.float32)
        scores = jnp.einsum('rkgd,skd->kgrs', query_tile.astype(jnp.float32), keys_here)
        highest = lax.optimization_barrier(jnp.max(scores, axis=-1, keepdims=True))
        weights = jnp.exp(scores - highest)
        totals = lax.optimization_barrier(jnp.sum(weights, axis=-1, keepdims=True))
        probs = weights.astype(jnp.bfloat16).astype(jnp.float32)
        mixed = jnp.einsum('kgrs,skd->kgrd', probs, values_here) / totals
        return jnp.transpose(mixed, (2, 0, 1, 3)).reshape(BLOCK, H * HD).astype(jnp.bfloat16)
    attended = lax.map(attend, (query_tiles, pattern)).reshape(QROWS, H * HD)
    return jnp.dot(attended, output_weight, preferred_element_type=jnp.float32).astype(jnp.bfloat16)
```

```python
import functools
import math

import jax
import jax.numpy as jnp
from jax import lax
from jax.experimental import pallas as pl
from jax.experimental.pallas import tpu as pltpu
from jax.sharding import PartitionSpec as P

HD = 128
BLOCK = 128
PIECES = 4
MESH = pl.DeviceIdType.MESH


def plain_device(hidden, norm_gain, query_weight, output_weight, cache, pattern):
    widened = hidden.astype(jnp.float32)
    meansq = jnp.mean(widened * widened, axis=-1, keepdims=True)
    normed = (widened * lax.rsqrt(meansq + 1e-05) * norm_gain.astype(jnp.float32)).astype(
        jnp.bfloat16
    )
    projected = jnp.dot(
        normed,
        lax.all_gather(query_weight, "corpus", axis=0, tiled=True),
        preferred_element_type=jnp.float32,
    )
    queries = (projected * (1.0 / math.sqrt(HD))).astype(jnp.bfloat16)
    kv_width = cache.shape[2]
    kv_heads = kv_width // HD
    head_local = query_weight.shape[1] // HD
    group_size = head_local // kv_heads
    query_blocks = pattern.shape[0]
    slot_total = query_blocks * pattern.shape[1]
    whole = lax.all_gather(cache, "corpus", axis=1, tiled=True)
    tiles = whole.reshape(2, whole.shape[1] // BLOCK, BLOCK, kv_width)
    picked = jnp.moveaxis(
        lax.map(
            lambda j: lax.dynamic_index_in_dim(tiles, j, axis=1, keepdims=False),
            pattern.reshape(slot_total),
        ),
        0,
        1,
    )
    key_span = pattern.shape[1] * BLOCK
    keys_here = picked[0].reshape(query_blocks, key_span, kv_heads, HD)
    values_here = picked[1].reshape(query_blocks, key_span, kv_heads, HD)
    query_tiles = queries.reshape(query_blocks, BLOCK, kv_heads, group_size, HD)
    scores = jnp.einsum(
        "qrkgd,qskd->qkgrs", query_tiles, keys_here, preferred_element_type=jnp.float32
    )
    highest = jnp.max(scores, axis=-1, keepdims=True)
    weights = jnp.exp(scores - highest)
    totals = jnp.sum(weights, axis=-1, keepdims=True)
    probs = weights.astype(jnp.bfloat16)
    mixed = (
        jnp.einsum("qkgrs,qskd->qkgrd", probs, values_here, preferred_element_type=jnp.float32)
        / totals
    )
    attended = (
        jnp.transpose(mixed, (0, 3, 1, 2, 4))
        .reshape(query_blocks * BLOCK, head_local * HD)
        .astype(jnp.bfloat16)
    )
    summed = lax.psum_scatter(
        jnp.dot(attended, output_weight, preferred_element_type=jnp.float32),
        "tensor",
        scatter_dimension=0,
        tiled=True,
    )
    return summed.astype(jnp.bfloat16)


def line_order(n):
    table = []
    for t in range(n):
        ups, downs = list(range(n - 1, t, -1)), list(range(t))
        first, second = (ups, downs) if len(ups) >= len(downs) else (downs, ups)
        row = []
        while first or second:
            if first:
                row.append(first.pop(0))
            if second:
                row.append(second.pop(0))
        table.append(row + [t])
    return table


def layer_kernel(
    n,
    n_corpus,
    hidden,
    gain,
    wq,
    wo,
    cache,
    pattern,
    out,
    hid,
    wg,
    wov,
    kv,
    acc,
    queries,
    kbuf,
    vbuf,
    att,
    part,
    up,
    down,
    snd,
    g_send,
    g_recv,
    l_sem,
    r_send,
    up_sem,
    down_sem,
):
    y, c, t = lax.axis_index("dp"), lax.axis_index("corpus"), lax.axis_index("tensor")
    x, core = c // 2, c % 2
    c_core = x * 2 + 1 - core
    c_x = (1 - x) * 2 + core
    c_xc = (1 - x) * 2 + 1 - core
    to_core, to_x, to_y = (y, c_core, t), (y, c_x, t), (1 - y, c, t)
    to_up, to_down = (y, c, t + 1), (y, c, t - 1)

    rows, kd = hid.shape[1], hid.shape[2]
    width = wq.shape[1]
    blk = cache.shape[1]

    hid_copies = [
        pltpu.make_async_copy(hidden.at[:, pl.ds(j * kd, kd)], hid.at[j], l_sem.at[j])
        for j in range(n_corpus)
    ]
    for cp in hid_copies:
        cp.start()
    w_copy = pltpu.make_async_copy(wq, wg.at[c], l_sem.at[n_corpus])
    kv_copy = pltpu.make_async_copy(cache, kv.at[:, pl.ds(c * blk, blk)], l_sem.at[n_corpus + 1])
    ncol = wov.shape[2]
    wo_copies = [
        pltpu.make_async_copy(
            wo.at[:, pl.ds(j * ncol, ncol)], wov.at[j], l_sem.at[n_corpus + 2 + j]
        )
        for j in range(wov.shape[0])
    ]
    w_copy.start()

    barrier = pltpu.get_barrier_semaphore()
    for partner in (to_core, to_x, to_y):
        pl.semaphore_signal(barrier, inc=1, device_id=partner, device_id_type=MESH)

    @pl.when(t > 0)
    def _():
        pl.semaphore_signal(barrier, inc=1, device_id=to_down, device_id_type=MESH)

    @pl.when(t < n - 1)
    def _():
        pl.semaphore_signal(barrier, inc=1, device_id=to_up, device_id_type=MESH)

    partners = 3 + jnp.where(t > 0, 1, 0) + jnp.where(t < n - 1, 1, 0)
    pl.semaphore_wait(barrier, partners)

    def remote(src, dst, which, kind, p, device):
        return pltpu.make_async_remote_copy(
            src_ref=src,
            dst_ref=dst,
            send_sem=g_send.at[which, kind, p],
            recv_sem=g_recv.at[which, kind, p],
            device_id=device,
            device_id_type=MESH,
        )

    w_rows = kd // 2 // PIECES
    kv_blk = blk // PIECES

    def w_piece(owner, half, p):
        return wg.at[owner, pl.ds(half * (kd // 2) + p * w_rows, w_rows)]

    def kv_piece(owner, half, p):
        first = owner * blk + half * (blk // 2) + (p % 2) * kv_blk
        return kv.at[p // 2, pl.ds(first, kv_blk)]

    def w_own(p):
        return wq.at[pl.ds(y * (kd // 2) + p * w_rows, w_rows)]

    def kv_own(p):
        return cache.at[p // 2, pl.ds(y * (blk // 2) + (p % 2) * kv_blk, kv_blk)]

    def x_send(which, p):
        own, piece = ((w_own, w_piece), (kv_own, kv_piece))[which]
        return remote(own(p), piece(c, y, p), which, 0, p, to_x)

    def y_send(which, p):
        piece = (w_piece, kv_piece)[which](c_x, y, p)
        return remote(piece, piece, which, 1, p, to_y)

    def cx_send(which, p):
        piece = (w_piece, kv_piece)[which](c_x, y, p)
        return remote(piece, piece, which, 3, p, to_core)

    def cy_send(which, p):
        piece = (w_piece, kv_piece)[which](c_x, 1 - y, p)
        return remote(piece, piece, which, 4, p, to_core)

    own_send = [
        remote(wq, wg.at[c], 0, 2, 0, to_core),
        remote(cache, kv.at[:, pl.ds(c * blk, blk)], 1, 2, 0, to_core),
    ]

    for p in range(PIECES):
        x_send(0, p).start()
    own_send[0].start()

    for cp in hid_copies:
        cp.wait()
    tile = 32

    def norm_rows(i, carry):
        at = pl.ds(pl.multiple_of(i * tile, tile), tile)
        total = jnp.zeros((tile, 1), jnp.float32)
        for j in range(n_corpus):
            wide = hid[j, at, :].astype(jnp.float32)
            total = total + jnp.sum(wide * wide, axis=1, keepdims=True)
        inv = lax.rsqrt(total * (1.0 / (n_corpus * kd)) + 1e-05)
        for j in range(n_corpus):
            wide = hid[j, at, :].astype(jnp.float32)
            scale = gain[:, j * kd : (j + 1) * kd].astype(jnp.float32)
            hid[j, at, :] = (wide * inv * scale).astype(jnp.bfloat16)
        return carry

    lax.fori_loop(0, rows // tile, norm_rows, 0)

    n_tile = 256

    def project(j, first):
        def body(i, carry):
            at = pl.ds(pl.multiple_of(i * n_tile, n_tile), n_tile)
            term = jnp.dot(hid[j], wg[j, :, at], preferred_element_type=jnp.float32)
            acc[:, at] = term if first else acc[:, at] + term
            return carry

        lax.fori_loop(0, width // n_tile, body, 0)

    w_copy.wait()
    project(c, True)
    kv_copy.start()
    own_send[1].start()
    for cp in wo_copies:
        cp.start()

    for p in range(PIECES):
        x_send(0, p).wait_recv()
        y_send(0, p).start()
        cx_send(0, p).start()
        x_send(1, p).start()
    own_send[0].wait_recv()
    project(c_core, False)
    for p in range(PIECES):
        y_send(0, p).wait_recv()
        cy_send(0, p).start()
    project(c_x, False)
    for p in range(PIECES):
        cx_send(0, p).wait_recv()
        cy_send(0, p).wait_recv()
    project(c_xc, False)
    heads = width // HD
    kv_heads = kv.shape[3] // HD
    group = heads // kv_heads
    blocks = rows // BLOCK
    for b in range(blocks):
        for h in range(heads):
            term = acc[b * BLOCK : (b + 1) * BLOCK, h * HD : (h + 1) * HD]
            queries[b, h] = (term * (1.0 / math.sqrt(HD))).astype(jnp.bfloat16)

    for p in range(PIECES):
        x_send(1, p).wait_recv()
        y_send(1, p).start()
        cx_send(1, p).start()
    for p in range(PIECES):
        y_send(1, p).wait_recv()
        cy_send(1, p).start()
    kv_copy.wait()
    own_send[1].wait_recv()
    for p in range(PIECES):
        cx_send(1, p).wait_recv()
        cy_send(1, p).wait_recv()
    for cp in wo_copies:
        cp.wait()

    slots = pattern.shape[1]
    together = 2
    table = line_order(n)
    n_parts = wov.shape[0]

    def passes(b, j):
        return pltpu.make_async_remote_copy(
            src_ref=snd.at[b, j],
            dst_ref=up.at[b, j],
            send_sem=r_send.at[b, j],
            recv_sem=up_sem.at[b, j],
            device_id=to_up,
            device_id_type=MESH,
        )

    def passes_down(b, j):
        return pltpu.make_async_remote_copy(
            src_ref=snd.at[b, j],
            dst_ref=down.at[b, j],
            send_sem=r_send.at[b, j],
            recv_sem=down_sem.at[b, j],
            device_id=to_down,
            device_id_type=MESH,
        )

    def one_block(step, carry):
        b = 0
        for i in range(n):
            for s in range(n):
                b = jnp.where((t == i) & (step == s), table[i][s], b)

        def pick(s, carry):
            block = pattern[b, s]
            at = pl.ds(pl.multiple_of(s * BLOCK, BLOCK), BLOCK)
            for h in range(kv_heads):
                kbuf[h, at, :] = kv[0, block, :, h * HD : (h + 1) * HD]
                vbuf[h, at, :] = kv[1, block, :, h * HD : (h + 1) * HD]
            return carry

        lax.fori_loop(0, slots, pick, 0)

        def attend(i, carry):
            h = i * together // group
            q = queries[b, pl.ds(i * together, together)].reshape(together * BLOCK, HD)
            scores = lax.dot_general(
                q, kbuf[h], (((1,), (1,)), ((), ())), preferred_element_type=jnp.float32
            )
            weights = jnp.exp(scores - jnp.max(scores, axis=1, keepdims=True))
            totals = jnp.sum(weights, axis=1, keepdims=True)
            mixed = jnp.dot(
                weights.astype(jnp.bfloat16), vbuf[h], preferred_element_type=jnp.float32
            )
            mixed = (mixed / totals).astype(jnp.bfloat16)
            att[pl.ds(i * together, together)] = mixed.reshape(together, BLOCK, HD)
            return carry

        lax.fori_loop(0, heads // together, attend, 0)

        def send_part(j, carry):
            left = jnp.concatenate([att[h] for h in range(heads)], axis=1)
            part[...] = jnp.dot(left, wov[j], preferred_element_type=jnp.float32)

            @pl.when((t > 0) & (b >= t))
            def _():
                passes(b, j).wait_recv()
                part[...] += up[b, j].astype(jnp.float32)

            @pl.when((t < n - 1) & (b <= t))
            def _():
                passes_down(b, j).wait_recv()
                part[...] += down[b, j].astype(jnp.float32)

            @pl.when(b > t)
            def _():
                snd[b, j] = part[...].astype(jnp.bfloat16)
                passes(b, j).start()

            @pl.when(b < t)
            def _():
                snd[b, j] = part[...].astype(jnp.bfloat16)
                passes_down(b, j).start()

            @pl.when(b == t)
            def _():
                out[:, pl.ds(pl.multiple_of(j * ncol, ncol), ncol)] = part[...].astype(
                    jnp.bfloat16
                )

            return carry

        lax.fori_loop(0, n_parts, send_part, 0)
        return carry

    lax.fori_loop(0, blocks, one_block, 0)

    for which in range(2):
        own_send[which].wait_send()
        for p in range(PIECES):
            for send in (x_send, y_send, cx_send, cy_send):
                send(which, p).wait_send()

    def finish(i, carry):
        b, j = i // n_parts, i % n_parts

        @pl.when(b > t)
        def _():
            passes(b, j).wait_send()

        @pl.when(b < t)
        def _():
            passes_down(b, j).wait_send()

        return carry

    lax.fori_loop(0, blocks * n_parts, finish, 0)


def fused_device(n, n_corpus, hidden, norm_gain, query_weight, output_weight, cache, pattern):
    rows, features = hidden.shape
    kd, width = query_weight.shape
    columns = output_weight.shape[1]
    kv_width = cache.shape[2]
    blk = cache.shape[1] // BLOCK
    heads = width // HD
    kv_heads = kv_width // HD
    blocks = rows // BLOCK
    span = pattern.shape[1] * BLOCK
    n_parts = 4
    ncol = columns // n_parts
    bf16, f32 = jnp.bfloat16, jnp.float32
    anywhere = pl.BlockSpec(memory_space=pl.ANY)
    vmem = pl.BlockSpec(memory_space=pltpu.VMEM)
    return pl.pallas_call(
        functools.partial(layer_kernel, n, n_corpus),
        out_shape=jax.ShapeDtypeStruct((rows // n, columns), bf16),
        in_specs=[
            anywhere,
            vmem,
            anywhere,
            anywhere,
            anywhere,
            pl.BlockSpec(memory_space=pltpu.SMEM),
        ],
        out_specs=vmem,
        scratch_shapes=[
            pltpu.VMEM((n_corpus, rows, kd), bf16),
            pltpu.VMEM((n_corpus, kd, width), bf16),
            pltpu.VMEM((n_parts, width, ncol), bf16),
            pltpu.VMEM((2, n_corpus * blk, BLOCK, kv_width), bf16),
            pltpu.VMEM((rows, width), f32),
            pltpu.VMEM((blocks, heads, BLOCK, HD), bf16),
            pltpu.VMEM((kv_heads, span, HD), bf16),
            pltpu.VMEM((kv_heads, span, HD), bf16),
            pltpu.VMEM((heads, BLOCK, HD), bf16),
            pltpu.VMEM((BLOCK, ncol), f32),
            pltpu.VMEM((n, n_parts, BLOCK, ncol), bf16),
            pltpu.VMEM((n, n_parts, BLOCK, ncol), bf16),
            pltpu.VMEM((n, n_parts, BLOCK, ncol), bf16),
            pltpu.SemaphoreType.DMA((2, 5, PIECES)),
            pltpu.SemaphoreType.DMA((2, 5, PIECES)),
            pltpu.SemaphoreType.DMA((n_corpus + 2 + n_parts,)),
            pltpu.SemaphoreType.DMA((n, n_parts)),
            pltpu.SemaphoreType.DMA((n, n_parts)),
            pltpu.SemaphoreType.DMA((n, n_parts)),
        ],
        compiler_params=pltpu.CompilerParams(
            collective_id=0, has_side_effects=True, vmem_limit_bytes=60 * 1024 * 1024
        ),
    )(
        hidden,
        norm_gain.reshape(1, features),
        query_weight,
        output_weight,
        cache.reshape(2, blk, BLOCK, kv_width),
        pattern,
    )


def solution(mesh):
    n_dp, n_corpus, n = mesh.shape["dp"], mesh.shape["corpus"], mesh.shape["tensor"]

    def per_device(hidden, norm_gain, query_weight, output_weight, cache, pattern):
        args = (hidden, norm_gain, query_weight, output_weight, cache, pattern)
        if n_dp == 2 and n_corpus == 4 and hidden.shape[0] == n * BLOCK:
            return fused_device(n, n_corpus, *args)
        return plain_device(*args)

    in_specs = (
        P(("dp", "corpus"), None),
        P(),
        P("corpus", "tensor"),
        P("tensor", None),
        P(None, "corpus", "tensor"),
        P(("dp", "corpus"), None),
    )
    out_specs = P(("dp", "corpus", "tensor"), None)
    return jax.shard_map(
        per_device, mesh=mesh, in_specs=in_specs, out_specs=out_specs, check_vma=False
    )
```

```python
import functools
import math

import jax
import jax.numpy as jnp
from jax import lax
from jax.experimental import pallas as pl
from jax.experimental.pallas import tpu as pltpu
from jax.sharding import PartitionSpec as P

HD = 128
BLOCK = 128
PIECES = 8
MESH = pl.DeviceIdType.MESH


def plain_device(hidden, norm_gain, query_weight, output_weight, cache, pattern):
    widened = hidden.astype(jnp.float32)
    meansq = jnp.mean(widened * widened, axis=-1, keepdims=True)
    normed = (widened * lax.rsqrt(meansq + 1e-05) * norm_gain.astype(jnp.float32)).astype(
        jnp.bfloat16
    )
    projected = jnp.dot(
        normed,
        lax.all_gather(query_weight, "corpus", axis=0, tiled=True),
        preferred_element_type=jnp.float32,
    )
    queries = (projected * (1.0 / math.sqrt(HD))).astype(jnp.bfloat16)
    kv_width = cache.shape[2]
    kv_heads = kv_width // HD
    head_local = query_weight.shape[1] // HD
    group_size = head_local // kv_heads
    query_blocks = pattern.shape[0]
    slot_total = query_blocks * pattern.shape[1]
    whole = lax.all_gather(cache, "corpus", axis=1, tiled=True)
    tiles = whole.reshape(2, whole.shape[1] // BLOCK, BLOCK, kv_width)
    picked = jnp.moveaxis(
        lax.map(
            lambda j: lax.dynamic_index_in_dim(tiles, j, axis=1, keepdims=False),
            pattern.reshape(slot_total),
        ),
        0,
        1,
    )
    key_span = pattern.shape[1] * BLOCK
    keys_here = picked[0].reshape(query_blocks, key_span, kv_heads, HD)
    values_here = picked[1].reshape(query_blocks, key_span, kv_heads, HD)
    query_tiles = queries.reshape(query_blocks, BLOCK, kv_heads, group_size, HD)
    scores = jnp.einsum(
        "qrkgd,qskd->qkgrs", query_tiles, keys_here, preferred_element_type=jnp.float32
    )
    highest = jnp.max(scores, axis=-1, keepdims=True)
    weights = jnp.exp(scores - highest)
    totals = jnp.sum(weights, axis=-1, keepdims=True)
    probs = weights.astype(jnp.bfloat16)
    mixed = (
        jnp.einsum("qkgrs,qskd->qkgrd", probs, values_here, preferred_element_type=jnp.float32)
        / totals
    )
    attended = (
        jnp.transpose(mixed, (0, 3, 1, 2, 4))
        .reshape(query_blocks * BLOCK, head_local * HD)
        .astype(jnp.bfloat16)
    )
    summed = lax.psum_scatter(
        jnp.dot(attended, output_weight, preferred_element_type=jnp.float32),
        "tensor",
        scatter_dimension=0,
        tiled=True,
    )
    return summed.astype(jnp.bfloat16)


def line_order(n):
    table = []
    for t in range(n):
        ups, downs = list(range(n - 1, t, -1)), list(range(t))
        first, second = (ups, downs) if len(ups) >= len(downs) else (downs, ups)
        row = []
        while first or second:
            if first:
                row.append(first.pop(0))
            if second:
                row.append(second.pop(0))
        table.append(row + [t])
    return table


def layer_kernel(
    n,
    n_corpus,
    hidden,
    gain,
    wq,
    wo,
    cache,
    pattern,
    out,
    hid,
    wg,
    wov,
    kv,
    acc,
    queries,
    kbuf,
    vbuf,
    att,
    part,
    up,
    down,
    snd,
    g_send,
    g_recv,
    l_sem,
    r_send,
    up_sem,
    down_sem,
):
    y, c, t = lax.axis_index("dp"), lax.axis_index("corpus"), lax.axis_index("tensor")
    x, core = c // 2, c % 2
    c_core = x * 2 + 1 - core
    c_x = (1 - x) * 2 + core
    c_xc = (1 - x) * 2 + 1 - core
    to_core, to_x, to_y = (y, c_core, t), (y, c_x, t), (1 - y, c, t)
    to_up, to_down = (y, c, t + 1), (y, c, t - 1)

    rows, kd = hid.shape[1], hid.shape[2]
    width = wq.shape[1]
    blk = cache.shape[1]

    hid_copies = [
        pltpu.make_async_copy(hidden.at[:, pl.ds(j * kd, kd)], hid.at[j], l_sem.at[j])
        for j in range(n_corpus)
    ]
    for cp in hid_copies:
        cp.start()
    w_copy = pltpu.make_async_copy(wq, wg.at[c], l_sem.at[n_corpus])
    kv_copy = pltpu.make_async_copy(cache, kv.at[:, pl.ds(c * blk, blk)], l_sem.at[n_corpus + 1])
    ncol = wov.shape[2]
    wo_copies = [
        pltpu.make_async_copy(
            wo.at[:, pl.ds(j * ncol, ncol)], wov.at[j], l_sem.at[n_corpus + 2 + j]
        )
        for j in range(wov.shape[0])
    ]
    w_copy.start()

    barrier = pltpu.get_barrier_semaphore()
    for partner in (to_core, to_x, to_y):
        pl.semaphore_signal(barrier, inc=1, device_id=partner, device_id_type=MESH)

    @pl.when(t > 0)
    def _():
        pl.semaphore_signal(barrier, inc=1, device_id=to_down, device_id_type=MESH)

    @pl.when(t < n - 1)
    def _():
        pl.semaphore_signal(barrier, inc=1, device_id=to_up, device_id_type=MESH)

    partners = 3 + jnp.where(t > 0, 1, 0) + jnp.where(t < n - 1, 1, 0)
    pl.semaphore_wait(barrier, partners)

    def remote(src, dst, which, kind, p, device):
        return pltpu.make_async_remote_copy(
            src_ref=src,
            dst_ref=dst,
            send_sem=g_send.at[which, kind, p],
            recv_sem=g_recv.at[which, kind, p],
            device_id=device,
            device_id_type=MESH,
        )

    w_rows = kd // 2 // PIECES
    kv_blk = blk // PIECES

    def w_piece(owner, half, p):
        return wg.at[owner, pl.ds(half * (kd // 2) + p * w_rows, w_rows)]

    def kv_piece(owner, half, p):
        first = owner * blk + half * (blk // 2) + (p % (PIECES // 2)) * kv_blk
        return kv.at[p // (PIECES // 2), pl.ds(first, kv_blk)]

    def w_own(p):
        return wq.at[pl.ds(y * (kd // 2) + p * w_rows, w_rows)]

    def kv_own(p):
        half = PIECES // 2
        return cache.at[p // half, pl.ds(y * (blk // 2) + (p % half) * kv_blk, kv_blk)]

    def x_send(which, p):
        own, piece = ((w_own, w_piece), (kv_own, kv_piece))[which]
        return remote(own(p), piece(c, y, p), which, 0, p, to_x)

    def y_send(which, p):
        piece = (w_piece, kv_piece)[which](c_x, y, p)
        return remote(piece, piece, which, 1, p, to_y)

    def cx_send(which, p):
        piece = (w_piece, kv_piece)[which](c_x, y, p)
        return remote(piece, piece, which, 3, p, to_core)

    def cy_send(which, p):
        piece = (w_piece, kv_piece)[which](c_x, 1 - y, p)
        return remote(piece, piece, which, 4, p, to_core)

    own_send = [
        remote(wq, wg.at[c], 0, 2, 0, to_core),
        remote(cache, kv.at[:, pl.ds(c * blk, blk)], 1, 2, 0, to_core),
    ]

    for p in range(PIECES):
        x_send(0, p).start()
    own_send[0].start()

    for cp in hid_copies:
        cp.wait()
    tile = 32

    def norm_rows(i, carry):
        at = pl.ds(pl.multiple_of(i * tile, tile), tile)
        total = jnp.zeros((tile, 1), jnp.float32)
        for j in range(n_corpus):
            wide = hid[j, at, :].astype(jnp.float32)
            total = total + jnp.sum(wide * wide, axis=1, keepdims=True)
        inv = lax.rsqrt(total * (1.0 / (n_corpus * kd)) + 1e-05)
        for j in range(n_corpus):
            wide = hid[j, at, :].astype(jnp.float32)
            scale = gain[:, j * kd : (j + 1) * kd].astype(jnp.float32)
            hid[j, at, :] = (wide * inv * scale).astype(jnp.bfloat16)
        return carry

    lax.fori_loop(0, rows // tile, norm_rows, 0)

    n_tile = 256

    def project(j, first):
        def body(i, carry):
            at = pl.ds(pl.multiple_of(i * n_tile, n_tile), n_tile)
            term = jnp.dot(hid[j], wg[j, :, at], preferred_element_type=jnp.float32)
            acc[:, at] = term if first else acc[:, at] + term
            return carry

        lax.fori_loop(0, width // n_tile, body, 0)

    w_copy.wait()
    project(c, True)
    kv_copy.start()
    own_send[1].start()
    for cp in wo_copies:
        cp.start()

    for p in range(PIECES):
        x_send(0, p).wait_recv()
        y_send(0, p).start()
        cx_send(0, p).start()
        x_send(1, p).start()
    own_send[0].wait_recv()
    project(c_core, False)
    for p in range(PIECES):
        y_send(0, p).wait_recv()
        cy_send(0, p).start()
    project(c_x, False)
    for p in range(PIECES):
        cx_send(0, p).wait_recv()
        cy_send(0, p).wait_recv()
    project(c_xc, False)
    heads = width // HD
    kv_heads = kv.shape[3] // HD
    group = heads // kv_heads
    blocks = rows // BLOCK
    for b in range(blocks):
        for h in range(heads):
            term = acc[b * BLOCK : (b + 1) * BLOCK, h * HD : (h + 1) * HD]
            queries[b, h] = (term * (1.0 / math.sqrt(HD))).astype(jnp.bfloat16)

    for p in range(PIECES):
        x_send(1, p).wait_recv()
        y_send(1, p).start()
        cx_send(1, p).start()
    for p in range(PIECES):
        y_send(1, p).wait_recv()
        cy_send(1, p).start()
    kv_copy.wait()
    own_send[1].wait_recv()
    for p in range(PIECES):
        cx_send(1, p).wait_recv()
        cy_send(1, p).wait_recv()
    for cp in wo_copies:
        cp.wait()

    slots = pattern.shape[1]
    together = 2
    table = line_order(n)
    n_parts = wov.shape[0]

    def passes(b, j):
        return pltpu.make_async_remote_copy(
            src_ref=snd.at[b, j],
            dst_ref=up.at[b, j],
            send_sem=r_send.at[b, j],
            recv_sem=up_sem.at[b, j],
            device_id=to_up,
            device_id_type=MESH,
        )

    def passes_down(b, j):
        return pltpu.make_async_remote_copy(
            src_ref=snd.at[b, j],
            dst_ref=down.at[b, j],
            send_sem=r_send.at[b, j],
            recv_sem=down_sem.at[b, j],
            device_id=to_down,
            device_id_type=MESH,
        )

    def one_block(step, carry):
        b = 0
        for i in range(n):
            for s in range(n):
                b = jnp.where((t == i) & (step == s), table[i][s], b)

        def pick(s, carry):
            block = pattern[b, s]
            at = pl.ds(pl.multiple_of(s * BLOCK, BLOCK), BLOCK)
            for h in range(kv_heads):
                kbuf[h, at, :] = kv[0, block, :, h * HD : (h + 1) * HD]
                vbuf[h, at, :] = kv[1, block, :, h * HD : (h + 1) * HD]
            return carry

        lax.fori_loop(0, slots, pick, 0)

        def attend(i, carry):
            h = i * together // group
            q = queries[b, pl.ds(i * together, together)].reshape(together * BLOCK, HD)
            scores = lax.dot_general(
                q, kbuf[h], (((1,), (1,)), ((), ())), preferred_element_type=jnp.float32
            )
            weights = jnp.exp(scores - jnp.max(scores, axis=1, keepdims=True))
            totals = jnp.sum(weights, axis=1, keepdims=True)
            mixed = jnp.dot(
                weights.astype(jnp.bfloat16), vbuf[h], preferred_element_type=jnp.float32
            )
            mixed = (mixed / totals).astype(jnp.bfloat16)
            att[pl.ds(i * together, together)] = mixed.reshape(together, BLOCK, HD)
            return carry

        lax.fori_loop(0, heads // together, attend, 0)

        def send_part(j, carry):
            left = jnp.concatenate([att[h] for h in range(heads)], axis=1)
            part[...] = jnp.dot(left, wov[j], preferred_element_type=jnp.float32)

            @pl.when((t > 0) & (b >= t))
            def _():
                passes(b, j).wait_recv()
                part[...] += up[b, j].astype(jnp.float32)

            @pl.when((t < n - 1) & (b <= t))
            def _():
                passes_down(b, j).wait_recv()
                part[...] += down[b, j].astype(jnp.float32)

            @pl.when(b > t)
            def _():
                snd[b, j] = part[...].astype(jnp.bfloat16)
                passes(b, j).start()

            @pl.when(b < t)
            def _():
                snd[b, j] = part[...].astype(jnp.bfloat16)
                passes_down(b, j).start()

            @pl.when(b == t)
            def _():
                out[:, pl.ds(pl.multiple_of(j * ncol, ncol), ncol)] = part[...].astype(
                    jnp.bfloat16
                )

            return carry

        lax.fori_loop(0, n_parts, send_part, 0)
        return carry

    lax.fori_loop(0, blocks, one_block, 0)

    for which in range(2):
        own_send[which].wait_send()
        for p in range(PIECES):
            for send in (x_send, y_send, cx_send, cy_send):
                send(which, p).wait_send()

    def finish(i, carry):
        b, j = i // n_parts, i % n_parts

        @pl.when(b > t)
        def _():
            passes(b, j).wait_send()

        @pl.when(b < t)
        def _():
            passes_down(b, j).wait_send()

        return carry

    lax.fori_loop(0, blocks * n_parts, finish, 0)


def fused_device(n, n_corpus, hidden, norm_gain, query_weight, output_weight, cache, pattern):
    rows, features = hidden.shape
    kd, width = query_weight.shape
    columns = output_weight.shape[1]
    kv_width = cache.shape[2]
    blk = cache.shape[1] // BLOCK
    heads = width // HD
    kv_heads = kv_width // HD
    blocks = rows // BLOCK
    span = pattern.shape[1] * BLOCK
    n_parts = 8
    ncol = columns // n_parts
    bf16, f32 = jnp.bfloat16, jnp.float32
    anywhere = pl.BlockSpec(memory_space=pl.ANY)
    vmem = pl.BlockSpec(memory_space=pltpu.VMEM)
    return pl.pallas_call(
        functools.partial(layer_kernel, n, n_corpus),
        out_shape=jax.ShapeDtypeStruct((rows // n, columns), bf16),
        in_specs=[
            anywhere,
            vmem,
            anywhere,
            anywhere,
            anywhere,
            pl.BlockSpec(memory_space=pltpu.SMEM),
        ],
        out_specs=vmem,
        scratch_shapes=[
            pltpu.VMEM((n_corpus, rows, kd), bf16),
            pltpu.VMEM((n_corpus, kd, width), bf16),
            pltpu.VMEM((n_parts, width, ncol), bf16),
            pltpu.VMEM((2, n_corpus * blk, BLOCK, kv_width), bf16),
            pltpu.VMEM((rows, width), f32),
            pltpu.VMEM((blocks, heads, BLOCK, HD), bf16),
            pltpu.VMEM((kv_heads, span, HD), bf16),
            pltpu.VMEM((kv_heads, span, HD), bf16),
            pltpu.VMEM((heads, BLOCK, HD), bf16),
            pltpu.VMEM((BLOCK, ncol), f32),
            pltpu.VMEM((n, n_parts, BLOCK, ncol), bf16),
            pltpu.VMEM((n, n_parts, BLOCK, ncol), bf16),
            pltpu.VMEM((n, n_parts, BLOCK, ncol), bf16),
            pltpu.SemaphoreType.DMA((2, 5, PIECES)),
            pltpu.SemaphoreType.DMA((2, 5, PIECES)),
            pltpu.SemaphoreType.DMA((n_corpus + 2 + n_parts,)),
            pltpu.SemaphoreType.DMA((n, n_parts)),
            pltpu.SemaphoreType.DMA((n, n_parts)),
            pltpu.SemaphoreType.DMA((n, n_parts)),
        ],
        compiler_params=pltpu.CompilerParams(
            collective_id=0, has_side_effects=True, vmem_limit_bytes=60 * 1024 * 1024
        ),
    )(
        hidden,
        norm_gain.reshape(1, features),
        query_weight,
        output_weight,
        cache.reshape(2, blk, BLOCK, kv_width),
        pattern,
    )


def solution(mesh):
    n_dp, n_corpus, n = mesh.shape["dp"], mesh.shape["corpus"], mesh.shape["tensor"]

    def per_device(hidden, norm_gain, query_weight, output_weight, cache, pattern):
        args = (hidden, norm_gain, query_weight, output_weight, cache, pattern)
        if n_dp == 2 and n_corpus == 4 and hidden.shape[0] == n * BLOCK:
            return fused_device(n, n_corpus, *args)
        return plain_device(*args)

    in_specs = (
        P(("dp", "corpus"), None),
        P(),
        P("corpus", "tensor"),
        P("tensor", None),
        P(None, "corpus", "tensor"),
        P(("dp", "corpus"), None),
    )
    out_specs = P(("dp", "corpus", "tensor"), None)
    return jax.shard_map(
        per_device, mesh=mesh, in_specs=in_specs, out_specs=out_specs, check_vma=False
    )
```
